32 devices in a mesh: slot: 16 (over z, y, core), tp: 2 (over x).
Axes of the slice: x: 2, y: 2, z: 4, core: 2. Of those that a mesh axis runs over, the one named last changes fastest.
Arguments:
- hidden: bfloat16 [7168, 6144], P('slot', 'tp'), may hold values from -4 to 4
- queries: bfloat16 [7168, 3072], P('slot', 'tp'), may hold values from -22 to 22
- key_rows: bfloat16 [7168, 3072], P('slot', 'tp'), may hold values from -6 to 6
- values: bfloat16 [7168, 3072], P('slot', 'tp'), may hold values from -6 to 6
- out_weight: bfloat16 [3072, 6144], P('tp'), may hold values from -0.109375 to 0.109375
- level_table: float32 [64, 6144], P(None, 'tp'), may hold values from 0.3 to 3
- noise_level: int32 [16], P('slot'), may hold values from 0 to 63
- group_live: int32 [16], replicated, may hold values 0 or 1
Outputs:
- refined: bfloat16 [7168, 6144], P('slot', 'tp')
The draws below stay inside these ranges and needn't reach their ends.
All inputs are finite; a program needn't handle non-finite values.
Results may differ from the reference program's by a relative error of at most 0.014.
Values may be sent and summed in bfloat16 or wider, within the bound.
A program may use at most 192 MiB of HBM per device.

```python
import math
import jax
import jax.numpy as jnp
from jax import lax

D = 6144
HEADS = 24
HD = 128
LEVELS = 64
GROUP = 448
TOKENS = 7168
N_SLOT = 16


def draw_key_rows(key, part):
    key = jax.random.fold_in(key, 1)
    drawn_draw = jnp.clip(jax.random.normal(key, (TOKENS, HEADS * HD), jnp.float32), -6.0, 6.0)
    return drawn_draw.astype(jnp.bfloat16)


def draw_queries(key, part):
    key = jax.random.fold_in(key, 2)
    drawn_draw = jnp.clip(2.5 * jax.random.normal(key, (TOKENS, HEADS * HD), jnp.float32), -15.0, 15.0)
    return drawn_draw.astype(jnp.bfloat16)


def touch_ends(result, key, smallest, largest):
    longest = result.shape.index(max(result.shape))
    spots = []
    for shift in (0, 1):
        where = [jax.random.randint(jax.random.fold_in(key, axis), (), 0, length) for axis, length in enumerate(result.shape)]
        where[longest] = (where[longest] + shift) % result.shape[longest]
        spots.append(tuple(where))
    return result.at[spots[0]].set(smallest).at[spots[1]].set(largest)


def block_levels(key, extent, cuts, low, top_value):
    gain = 1.0
    for position, parts in cuts:
        steps = jax.random.uniform(jax.random.fold_in(jax.random.fold_in(key, 6), position), (parts,), jnp.float32, low / len(cuts), top_value / len(cuts))
        gain = gain * jnp.repeat(jnp.exp(steps), extent[position] // parts).reshape((-1,) + (1,) * (len(extent) - 1 - position))
    return gain


def noise(own_key, dims, spread, limit, pieces=(), dtype=jnp.bfloat16):
    drawn = spread * jax.random.normal(own_key, dims, jnp.float32)
    if pieces:
        drawn = drawn * block_levels(own_key, dims, pieces, -0.22, 0.18)
    return jnp.clip(drawn, -limit, limit).astype(dtype)


def setup_inputs(seed: int = 0) -> dict:
    splits = jax.random.split(jax.random.key(seed), 9)
    hidden = noise(splits[0], (TOKENS, D), 0.5, 4.0, ((0, 16), (1, 2)))
    queries = draw_queries(jax.random.fold_in(splits[8], 71), 0)
    key_rows = draw_key_rows(jax.random.fold_in(splits[8], 71), 0)
    values = noise(splits[3], (TOKENS, HEADS * HD), 1.0, 6.0, ((0, 16), (1, 2)))
    out_weight = noise(splits[4], (HEADS * HD, D), (HEADS * HD) ** -0.5, 0.109375, ((0, 2),))
    level_table = jnp.clip(jnp.exp(math.log(3.0) - 2.3025851 * jax.random.uniform(splits[5], (LEVELS, D), jnp.float32) ** block_levels(splits[5], (LEVELS, D), ((1, 2),), -0.2, 0.2)), 0.3, 3.0)
    noise_level = touch_ends(jax.random.randint(splits[6], (N_SLOT,), 0, LEVELS), jax.random.fold_in(splits[6], 1), 0, LEVELS - 1).astype(jnp.int32)
    group_live = touch_ends((jax.random.randint(splits[7], (N_SLOT,), 0, 4) < 3).astype(jnp.int32), jax.random.fold_in(splits[7], 1), 0, 1)
    return {"hidden": hidden, "queries": queries, "key_rows": key_rows, "values": values, "out_weight": out_weight, "level_table": level_table, "noise_level": noise_level, "group_live": group_live}


def reference(hidden, queries, key_rows, values, out_weight, level_table, noise_level, group_live):
    score_scale = HD ** -0.5
    pieces_out = []
    for slot_index in range(N_SLOT):
        span_end = (slot_index + 1) * GROUP
        query_part = queries[slot_index * GROUP:span_end].reshape(GROUP, HEADS, HD).transpose(1, 0, 2)
        key_part = key_rows[:span_end].reshape(span_end, HEADS, HD).transpose(1, 0, 2)
        value_part = values[:span_end].reshape(span_end, HEADS, HD).transpose(1, 0, 2)
        group_of = jnp.arange(span_end) // GROUP
        allowed = (group_live[group_of] == 1) | (group_of == slot_index)

        def one_head(operands):
            query_head, key_head, value_head = operands
            scores = jnp.dot(query_head, key_head.T, preferred_element_type=jnp.float32) * score_scale
            masked = jnp.where(allowed[None, :], scores, -1e30)
            rowmax = jnp.max(masked, axis=1, keepdims=True)
            expon = jnp.where(allowed[None, :], jnp.exp(scores - rowmax), 0.0)
            rowsum = jnp.sum(expon, axis=1, keepdims=True)
            mixed_head = jnp.dot(expon.astype(jnp.bfloat16), value_head, preferred_element_type=jnp.float32) / rowsum
            return mixed_head.astype(jnp.bfloat16)

        per_head = lax.map(one_head, (query_part, key_part, value_part))
        pieces_out.append(per_head.transpose(1, 0, 2).reshape(GROUP, HEADS * HD))
    attended = jnp.concatenate(pieces_out, axis=0)
    projected = jnp.dot(attended, out_weight, preferred_element_type=jnp.float32)
    gate_row = jnp.repeat(level_table[noise_level], GROUP, axis=0)
    mixed_out = (hidden.astype(jnp.float32) + gate_row * projected).astype(jnp.bfloat16)
    return jnp.roll(mixed_out, -GROUP, axis=0)
```

```python
import math

import jax
import jax.numpy as jnp
from jax import lax
from jax.experimental import pallas as pl
from jax.experimental.pallas import tpu as pltpu
from jax.sharding import PartitionSpec as P

HD = 128
EXP2_SCALE = HD ** (-0.5) * math.log2(math.e)


def passed_along(value, axis, steps):
    count = lax.axis_size(axis)
    pairs = [(source, (source + steps) % count) for source in range(count)]
    return lax.ppermute(value, axis, pairs)


def swapped_with_pair(value):
    count = lax.axis_size("slot")
    return lax.ppermute(value, "slot", [(source, source ^ 1) for source in range(count)])


def attend_kernel(order_ref, count_ref, query_ref, kv_ref, out_ref, top, total, weighted):
    step = pl.program_id(0)
    width = query_ref.shape[1]
    heads = width // HD

    @pl.when(step == 0)
    def _():
        top[...] = jnp.full(top.shape, -1e30, jnp.float32)
        total[...] = jnp.zeros(total.shape, jnp.float32)
        weighted[...] = jnp.zeros(weighted.shape, jnp.float32)

    @pl.when(step < count_ref[0])
    def _():
        for head in range(heads):
            low = head * HD
            scores = lax.dot_general(
                query_ref[:, low : low + HD],
                kv_ref[:, low : low + HD],
                (((1,), (1,)), ((), ())),
                preferred_element_type=jnp.float32,
            )
            old_top = top[head]
            new_top = jnp.maximum(old_top, jnp.max(scores, axis=1, keepdims=True))
            expon = jnp.exp2((scores - new_top) * EXP2_SCALE)
            shrink = jnp.exp2((old_top - new_top) * EXP2_SCALE)
            total[head] = total[head] * shrink + jnp.sum(expon, axis=1, keepdims=True)
            weighted[head] = weighted[head] * shrink + jnp.dot(
                expon.astype(jnp.bfloat16),
                kv_ref[:, width + low : width + low + HD],
                preferred_element_type=jnp.float32,
            )
            top[head] = new_top

    @pl.when(step == pl.num_programs(0) - 1)
    def _():
        for head in range(heads):
            out_ref[:, head * HD : (head + 1) * HD] = (weighted[head] / total[head]).astype(
                out_ref.dtype
            )


def attend(order, count, queries, gathered, groups):
    rows, width = queries.shape
    heads = width // HD
    pairs = rows * gathered.shape[0] * heads
    return pl.pallas_call(
        attend_kernel,
        out_shape=jax.ShapeDtypeStruct((rows, width), jnp.bfloat16),
        grid_spec=pltpu.PrefetchScalarGridSpec(
            num_scalar_prefetch=2,
            grid=(groups,),
            in_specs=[
                pl.BlockSpec((rows, width), lambda step, order, count: (0, 0)),
                pl.BlockSpec((rows, 2 * width), lambda step, order, count: (order[step], 0)),
            ],
            out_specs=pl.BlockSpec((rows, width), lambda step, order, count: (0, 0)),
            scratch_shapes=[
                pltpu.VMEM((heads, rows, 1), jnp.float32),
                pltpu.VMEM((heads, rows, 1), jnp.float32),
                pltpu.VMEM((heads, rows, HD), jnp.float32),
            ],
        ),
        compiler_params=pltpu.CompilerParams(vmem_limit_bytes=56 * 1024 * 1024),
        cost_estimate=pl.CostEstimate(
            flops=4 * pairs * HD,
            bytes_accessed=gathered.size * 2 + 4 * rows * width,
            transcendentals=pairs,
        ),
    )(order, count, queries, gathered)


def head_chunks(heads):
    last = max(1, heads // 6)
    middle = heads // 3
    return [heads - middle - last, middle, last]


def per_device(hidden, queries, key_rows, values, out_weight, level_table, noise_level, group_live):
    rows, width = queries.shape
    out_width = hidden.shape[1]
    groups = lax.axis_size("slot")
    shards = lax.axis_size("tp")
    own_slot = lax.axis_index("slot")
    own_shard = lax.axis_index("tp")
    group = lax.rem(own_slot + 1, groups)

    spans = []
    start = 0
    for heads in head_chunks(width // HD):
        spans.append((start, start + heads * HD))
        start += heads * HD
    queries = passed_along(queries, "slot", -1)
    level = passed_along(noise_level, "slot", -1)
    hidden = passed_along(hidden, "slot", -1)

    gathered = []
    for place, (low, high) in enumerate(spans):
        piece = jnp.concatenate([key_rows[:, low:high], values[:, low:high]], axis=1)
        if place == 1:
            piece, queries = lax.optimization_barrier((piece, queries))
        elif place > 1:
            piece, gathered[-2] = lax.optimization_barrier((piece, gathered[-2]))
        gathered.append(lax.all_gather(piece, "slot", axis=0, tiled=True))

    half = width // 2
    parity = lax.rem(own_slot, 2)
    weights = [lax.dynamic_slice(out_weight, (0, own_shard * out_width), (width, out_width))]
    for shift in range(1, shards):
        target = lax.rem(own_shard + shift, shards)
        sent = lax.dynamic_slice(
            out_weight, (parity * half, target * out_width), (half, out_width)
        )
        mine = passed_along(sent, "tp", shift)
        other = swapped_with_pair(mine)
        weights.append(
            jnp.concatenate(
                [jnp.where(parity == 0, mine, other), jnp.where(parity == 0, other, mine)], axis=0
            )
        )

    slot_ids = jnp.arange(groups, dtype=jnp.int32)
    needed = ((slot_ids < group) & (group_live == 1)) | (slot_ids == group)
    place = jnp.cumsum(needed.astype(jnp.int32)) - 1
    count = jnp.sum(needed.astype(jnp.int32))
    hits = needed[None, :] & (place[None, :] == slot_ids[:, None])
    order = jnp.where(
        slot_ids < count, jnp.sum(jnp.where(hits, slot_ids[None, :], 0), axis=1), group
    ).astype(jnp.int32)
    count = count.reshape(1)

    projected = jnp.zeros((rows, out_width), jnp.float32)
    for (low, high), piece in zip(spans, gathered):
        attended = attend(order, count, queries[:, low:high], piece, groups)
        attended, queries = lax.optimization_barrier((attended, queries))
        received = [attended] + [passed_along(attended, "tp", shift) for shift in range(1, shards)]
        for block, weight in zip(received, weights):
            projected = projected + jnp.dot(
                block, weight[low:high], preferred_element_type=jnp.float32
            )

    picked = jnp.arange(level_table.shape[0], dtype=jnp.int32) == level[0]
    gate_row = jnp.sum(jnp.where(picked[:, None], level_table, 0.0), axis=0)
    return (hidden.astype(jnp.float32) + gate_row[None, :] * projected).astype(jnp.bfloat16)


def solution(mesh):
    in_specs = (
        P("slot", "tp"),
        P("slot", "tp"),
        P("slot", "tp"),
        P("slot", "tp"),
        P("tp", None),
        P(None, "tp"),
        P("slot"),
        P(),
    )
    out_specs = P("slot", "tp")
    return jax.shard_map(
        per_device, mesh=mesh, in_specs=in_specs, out_specs=out_specs, check_vma=False
    )
```

```python
import math

import jax
import jax.numpy as jnp
from jax import lax
from jax.experimental import pallas as pl
from jax.experimental.pallas import tpu as pltpu
from jax.sharding import PartitionSpec as P

HD = 128
EXP2_SCALE = HD ** (-0.5) * math.log2(math.e)


def passed_along(value, axis, steps):
    count = lax.axis_size(axis)
    pairs = [(source, (source + steps) % count) for source in range(count)]
    return lax.ppermute(value, axis, pairs)


def swapped_with_pair(value):
    count = lax.axis_size("slot")
    return lax.ppermute(value, "slot", [(source, source ^ 1) for source in range(count)])


def attend_kernel(order_ref, count_ref, query_ref, kv_ref, out_ref, top, total, weighted):
    step = pl.program_id(0)
    width = query_ref.shape[1]
    heads = width // HD

    @pl.when(step == 0)
    def _():
        top[...] = jnp.full(top.shape, -1e30, jnp.float32)
        total[...] = jnp.zeros(total.shape, jnp.float32)
        weighted[...] = jnp.zeros(weighted.shape, jnp.float32)

    @pl.when(step < count_ref[0])
    def _():
        for head in range(heads):
            low = head * HD
            scores = lax.dot_general(
                kv_ref[:, low : low + HD],
                query_ref[:, low : low + HD],
                (((1,), (1,)), ((), ())),
                preferred_element_type=jnp.float32,
            )
            old_top = top[head]
            new_top = jnp.maximum(old_top, jnp.max(scores, axis=0, keepdims=True))
            expon = jnp.exp2((scores - new_top) * EXP2_SCALE)
            shrink = jnp.exp2((old_top - new_top) * EXP2_SCALE)
            total[head] = total[head] * shrink + jnp.sum(expon, axis=0, keepdims=True)
            weighted[head] = weighted[head] * shrink + lax.dot_general(
                kv_ref[:, width + low : width + low + HD],
                expon.astype(jnp.bfloat16),
                (((0,), (0,)), ((), ())),
                preferred_element_type=jnp.float32,
            )
            top[head] = new_top

    @pl.when(step == pl.num_programs(0) - 1)
    def _():
        for head in range(heads):
            out_ref[:, head * HD : (head + 1) * HD] = (
                (weighted[head] / total[head]).T.astype(out_ref.dtype)
            )


def attend(order, count, queries, gathered, groups):
    rows, width = queries.shape
    heads = width // HD
    pairs = rows * gathered.shape[0] * heads
    return pl.pallas_call(
        attend_kernel,
        out_shape=jax.ShapeDtypeStruct((rows, width), jnp.bfloat16),
        grid_spec=pltpu.PrefetchScalarGridSpec(
            num_scalar_prefetch=2,
            grid=(groups,),
            in_specs=[
                pl.BlockSpec((rows, width), lambda step, order, count: (0, 0)),
                pl.BlockSpec((rows, 2 * width), lambda step, order, count: (order[step], 0)),
            ],
            out_specs=pl.BlockSpec((rows, width), lambda step, order, count: (0, 0)),
            scratch_shapes=[
                pltpu.VMEM((heads, 1, rows), jnp.float32),
                pltpu.VMEM((heads, 1, rows), jnp.float32),
                pltpu.VMEM((heads, HD, rows), jnp.float32),
            ],
        ),
        compiler_params=pltpu.CompilerParams(vmem_limit_bytes=56 * 1024 * 1024),
        cost_estimate=pl.CostEstimate(
            flops=4 * pairs * HD,
            bytes_accessed=gathered.size * 2 + 4 * rows * width,
            transcendentals=pairs,
        ),
    )(order, count, queries, gathered)


def per_device(hidden, queries, key_rows, values, out_weight, level_table, noise_level, group_live):
    rows, width = queries.shape
    out_width = hidden.shape[1]
    groups = lax.axis_size("slot")
    shards = lax.axis_size("tp")
    own_slot = lax.axis_index("slot")
    own_shard = lax.axis_index("tp")
    group = lax.rem(own_slot + 1, groups)

    heads = width // HD
    cut = (heads - max(1, heads // 4)) * HD

    def gather(low, high, after=None):
        piece = jnp.concatenate([key_rows[:, low:high], values[:, low:high]], axis=1)
        if after is not None:
            piece, after = lax.optimization_barrier((piece, after))
        return lax.all_gather(piece, "slot", axis=0, tiled=True), after

    first, _ = gather(0, cut)
    level = passed_along(noise_level, "slot", -1)
    queries = passed_along(queries, "slot", -1)
    second, (queries, level) = gather(cut, width, (queries, level))

    half = width // 2
    parity = lax.rem(own_slot, 2)
    own_weight = lax.dynamic_slice(out_weight, (0, own_shard * out_width), (width, out_width))
    halves = []
    for shift in range(1, shards):
        target = lax.rem(own_shard + shift, shards)
        sent = lax.dynamic_slice(
            out_weight, (parity * half, target * out_width), (half, out_width)
        )
        halves.append(passed_along(sent, "tp", shift))

    slot_ids = jnp.arange(groups, dtype=jnp.int32)
    needed = ((slot_ids < group) & (group_live == 1)) | (slot_ids == group)
    place = jnp.cumsum(needed.astype(jnp.int32)) - 1
    count = jnp.sum(needed.astype(jnp.int32))
    hits = needed[None, :] & (place[None, :] == slot_ids[:, None])
    order = jnp.where(
        slot_ids < count, jnp.sum(jnp.where(hits, slot_ids[None, :], 0), axis=1), group
    ).astype(jnp.int32)
    count = count.reshape(1)

    def shared(attended):
        others = [passed_along(attended, "tp", shift) for shift in range(1, shards)]
        return jnp.concatenate([attended] + others, axis=1)

    attended = attend(order, count, queries[:, :cut], first, groups)
    attended, queries, halves = lax.optimization_barrier((attended, queries, halves))
    weights = [own_weight]
    for mine in halves:
        other = swapped_with_pair(mine)
        weights += [
            jnp.concatenate(
                [jnp.where(parity == 0, mine, other), jnp.where(parity == 0, other, mine)], axis=0
            )
        ]
    first_weight = jnp.concatenate([weight[:cut] for weight in weights], axis=0)
    second_weight = jnp.concatenate([weight[cut:] for weight in weights], axis=0)
    projected = jnp.dot(shared(attended), first_weight, preferred_element_type=jnp.float32)
    picked = jnp.arange(level_table.shape[0], dtype=jnp.int32) == level[0]
    gate_row = jnp.sum(jnp.where(picked[:, None], level_table, 0.0), axis=0)

    hidden, _ = lax.optimization_barrier((hidden, second[:16, :HD]))
    queries, projected, second_weight = lax.optimization_barrier(
        (queries, projected, second_weight)
    )
    hidden = passed_along(hidden, "slot", -1)
    attended = attend(order, count, queries[:, cut:], second, groups)
    projected = projected + jnp.dot(
        shared(attended), second_weight, preferred_element_type=jnp.float32
    )
    return (hidden.astype(jnp.float32) + gate_row[None, :] * projected).astype(jnp.bfloat16)


def solution(mesh):
    in_specs = (
        P("slot", "tp"),
        P("slot", "tp"),
        P("slot", "tp"),
        P("slot", "tp"),
        P("tp", None),
        P(None, "tp"),
        P("slot"),
        P(),
    )
    out_specs = P("slot", "tp")
    return jax.shard_map(
        per_device, mesh=mesh, in_specs=in_specs, out_specs=out_specs, check_vma=False
    )
```

```python
import math

import jax
import jax.numpy as jnp
from jax import lax
from jax.experimental import pallas as pl
from jax.experimental.pallas import tpu as pltpu
from jax.sharding import PartitionSpec as P

HD = 128
EXP2_SCALE = HD ** (-0.5) * math.log2(math.e)


def passed_along(value, axis, steps):
    count = lax.axis_size(axis)
    pairs = [(source, (source + steps) % count) for source in range(count)]
    return lax.ppermute(value, axis, pairs)


def swapped_with_pair(value):
    count = lax.axis_size("slot")
    return lax.ppermute(value, "slot", [(source, source ^ 1) for source in range(count)])


def attend_kernel(order_ref, count_ref, query_ref, kv_ref, mark_ref, out_ref, top, total, weighted):
    step = pl.program_id(0)
    width = query_ref.shape[1]
    heads = width // HD

    @pl.when(step == 0)
    def _():
        top[...] = jnp.full(top.shape, -1e30, jnp.float32)
        total[...] = jnp.zeros(total.shape, jnp.float32)
        weighted[...] = jnp.zeros(weighted.shape, jnp.float32)

    @pl.when(step < count_ref[0])
    def _():
        def score(head):
            low = head * HD
            return lax.dot_general(
                kv_ref[:, low : low + HD],
                query_ref[:, low : low + HD],
                (((1,), (1,)), ((), ())),
                preferred_element_type=jnp.float32,
            )

        upcoming = score(0)
        for head in range(heads):
            low = head * HD
            scores = upcoming
            if head + 1 < heads:
                upcoming = score(head + 1)
            old_top = top[head]
            new_top = jnp.maximum(old_top, jnp.max(scores, axis=0, keepdims=True))
            expon = jnp.exp2((scores - new_top) * EXP2_SCALE)
            shrink = jnp.exp2((old_top - new_top) * EXP2_SCALE)
            total[head] = total[head] * shrink + jnp.sum(expon, axis=0, keepdims=True)
            weighted[head] = weighted[head] * shrink + lax.dot_general(
                kv_ref[:, width + low : width + low + HD],
                expon.astype(jnp.bfloat16),
                (((0,), (0,)), ((), ())),
                preferred_element_type=jnp.float32,
            )
            top[head] = new_top

    @pl.when(step == pl.num_programs(0) - 1)
    def _():
        for head in range(heads):
            out_ref[:, head * HD : (head + 1) * HD] = (
                (weighted[head] / total[head]).T.astype(out_ref.dtype)
            )


def attend(order, count, queries, gathered, mark, groups):
    rows, width = queries.shape
    heads = width // HD
    pairs = rows * gathered.shape[0] * heads
    return pl.pallas_call(
        attend_kernel,
        out_shape=jax.ShapeDtypeStruct((rows, width), jnp.bfloat16),
        grid_spec=pltpu.PrefetchScalarGridSpec(
            num_scalar_prefetch=2,
            grid=(groups,),
            in_specs=[
                pl.BlockSpec((rows, width), lambda step, order, count: (0, 0)),
                pl.BlockSpec((rows, 2 * width), lambda step, order, count: (order[step], 0)),
                pl.BlockSpec(mark.shape, lambda step, order, count: (0, 0)),
            ],
            out_specs=pl.BlockSpec((rows, width), lambda step, order, count: (0, 0)),
            scratch_shapes=[
                pltpu.VMEM((heads, 1, rows), jnp.float32),
                pltpu.VMEM((heads, 1, rows), jnp.float32),
                pltpu.VMEM((heads, HD, rows), jnp.float32),
            ],
        ),
        compiler_params=pltpu.CompilerParams(vmem_limit_bytes=56 * 1024 * 1024),
        cost_estimate=pl.CostEstimate(
            flops=4 * pairs * HD,
            bytes_accessed=gathered.size * 2 + 4 * rows * width,
            transcendentals=pairs,
        ),
    )(order, count, queries, gathered, mark)


def per_device(hidden, queries, key_rows, values, out_weight, level_table, noise_level, group_live):
    rows, width = queries.shape
    out_width = hidden.shape[1]
    groups = lax.axis_size("slot")
    shards = lax.axis_size("tp")
    own_slot = lax.axis_index("slot")
    own_shard = lax.axis_index("tp")
    group = lax.rem(own_slot + 1, groups)

    heads = width // HD
    cut = (heads - max(1, heads // 4)) * HD

    def joined(low, high):
        return jnp.concatenate([key_rows[:, low:high], values[:, low:high]], axis=1)

    first = lax.all_gather(joined(0, cut), "slot", axis=0, tiled=True)
    first_mark = first[:16, :HD]
    level = passed_along(noise_level, "slot", -1)
    queries = passed_along(queries, "slot", -1)

    half = width // 2
    parity = lax.rem(own_slot, 2)
    own_weight = lax.dynamic_slice(out_weight, (0, own_shard * out_width), (width, out_width))
    weights = [own_weight]
    for shift in range(1, shards):
        target = lax.rem(own_shard + shift, shards)
        sent = lax.dynamic_slice(
            out_weight, (parity * half, target * out_width), (half, out_width)
        )
        mine = passed_along(sent, "tp", shift)
        mine, queries, level = lax.optimization_barrier((mine, queries, level))
        other = swapped_with_pair(mine)
        weights.append(
            jnp.concatenate(
                [jnp.where(parity == 0, mine, other), jnp.where(parity == 0, other, mine)], axis=0
            )
        )
    first_weight = jnp.concatenate([own_weight] + [weight[:cut] for weight in weights[1:]], axis=0)
    second_weight = jnp.concatenate([weight[cut:] for weight in weights[1:]], axis=0)
    piece, first_mark, queries, first_weight, second_weight = lax.optimization_barrier(
        (joined(cut, width), first_mark, queries, first_weight, second_weight)
    )
    second = lax.all_gather(piece, "slot", axis=0, tiled=True)
    second_mark = second[:16, :HD]

    slot_ids = jnp.arange(groups, dtype=jnp.int32)
    needed = ((slot_ids < group) & (group_live == 1)) | (slot_ids == group)
    place = jnp.cumsum(needed.astype(jnp.int32)) - 1
    count = jnp.sum(needed.astype(jnp.int32))
    hits = needed[None, :] & (place[None, :] == slot_ids[:, None])
    order = jnp.where(
        slot_ids < count, jnp.sum(jnp.where(hits, slot_ids[None, :], 0), axis=1), group
    ).astype(jnp.int32)
    count = count.reshape(1)

    def from_others(attended):
        return [passed_along(attended, "tp", shift) for shift in range(1, shards)]

    picked = jnp.arange(level_table.shape[0], dtype=jnp.int32) == level[0]
    gate_row = jnp.sum(jnp.where(picked[:, None], level_table, 0.0), axis=0)

    attended = attend(order, count, queries[:, :cut], first, first_mark, groups)
    attended, queries, gate_row = lax.optimization_barrier((attended, queries, gate_row))
    received = from_others(attended)
    second_mark, hidden, attended = lax.optimization_barrier((second_mark, hidden, attended))
    hidden = passed_along(hidden, "slot", -1)
    last = attend(order, count, queries[:, cut:], second, second_mark, groups)
    last_received = from_others(last)
    projected = jnp.dot(
        jnp.concatenate([attended, last] + received, axis=1),
        first_weight,
        preferred_element_type=jnp.float32,
    )
    projected = projected + jnp.dot(
        jnp.concatenate(last_received, axis=1), second_weight, preferred_element_type=jnp.float32
    )
    return (hidden.astype(jnp.float32) + gate_row[None, :] * projected).astype(jnp.bfloat16)


def solution(mesh):
    in_specs = (
        P("slot", "tp"),
        P("slot", "tp"),
        P("slot", "tp"),
        P("slot", "tp"),
        P("tp", None),
        P(None, "tp"),
        P("slot"),
        P(),
    )
    out_specs = P("slot", "tp")
    return jax.shard_map(
        per_device, mesh=mesh, in_specs=in_specs, out_specs=out_specs, check_vma=False
    )
```

```python
import math

import jax
import jax.numpy as jnp
from jax import lax
from jax.experimental import pallas as pl
from jax.experimental.pallas import tpu as pltpu
from jax.sharding import PartitionSpec as P

HD = 128
EXP2_SCALE = HD ** (-0.5) * math.log2(math.e)


def passed_along(value, axis, steps):
    count = lax.axis_size(axis)
    pairs = [(source, (source + steps) % count) for source in range(count)]
    return lax.ppermute(value, axis, pairs)


def swapped_with_pair(value):
    count = lax.axis_size("slot")
    return lax.ppermute(value, "slot", [(source, source ^ 1) for source in range(count)])


def attend_kernel(order_ref, count_ref, query_ref, kv_ref, next_ref, mark_ref, out_ref, top, total, weighted):
    step = pl.program_id(0)
    width = query_ref.shape[1]
    heads = width // HD

    @pl.when(step == 0)
    def _():
        top[...] = jnp.full(top.shape, -1e30, jnp.float32)
        total[...] = jnp.zeros(total.shape, jnp.float32)
        weighted[...] = jnp.zeros(weighted.shape, jnp.float32)

    def absorb(blocks):
        units = [(block, head) for block in blocks for head in range(heads)]

        def score(unit):
            block, head = unit
            low = head * HD
            return lax.dot_general(
                block[:, low : low + HD],
                query_ref[:, low : low + HD],
                (((1,), (1,)), ((), ())),
                preferred_element_type=jnp.float32,
            )

        upcoming = score(units[0])
        for place, (block, head) in enumerate(units):
            low = head * HD
            scores = upcoming
            if place + 1 < len(units):
                upcoming = score(units[place + 1])
            old_top = top[head]
            new_top = jnp.maximum(old_top, jnp.max(scores, axis=0, keepdims=True))
            expon = jnp.exp2((scores - new_top) * EXP2_SCALE)
            shrink = jnp.exp2((old_top - new_top) * EXP2_SCALE)
            total[head] = total[head] * shrink + jnp.sum(expon, axis=0, keepdims=True)
            weighted[head] = weighted[head] * shrink + lax.dot_general(
                block[:, width + low : width + low + HD],
                expon.astype(jnp.bfloat16),
                (((0,), (0,)), ((), ())),
                preferred_element_type=jnp.float32,
            )
            top[head] = new_top

    @pl.when(2 * step + 1 < count_ref[0])
    def _():
        absorb([kv_ref, next_ref])

    @pl.when(2 * step + 1 == count_ref[0])
    def _():
        absorb([kv_ref])

    @pl.when(step == pl.num_programs(0) - 1)
    def _():
        for head in range(heads):
            out_ref[:, head * HD : (head + 1) * HD] = (
                (weighted[head] / total[head]).T.astype(out_ref.dtype)
            )


def attend(order, count, queries, gathered, mark, groups):
    rows, width = queries.shape
    heads = width // HD
    pairs = rows * gathered.shape[0] * heads
    return pl.pallas_call(
        attend_kernel,
        out_shape=jax.ShapeDtypeStruct((rows, width), jnp.bfloat16),
        grid_spec=pltpu.PrefetchScalarGridSpec(
            num_scalar_prefetch=2,
            grid=(groups // 2,),
            in_specs=[
                pl.BlockSpec((rows, width), lambda step, order, count: (0, 0)),
                pl.BlockSpec((rows, 2 * width), lambda step, order, count: (order[2 * step], 0)),
                pl.BlockSpec((rows, 2 * width), lambda step, order, count: (order[2 * step + 1], 0)),
                pl.BlockSpec(mark.shape, lambda step, order, count: (0, 0)),
            ],
            out_specs=pl.BlockSpec((rows, width), lambda step, order, count: (0, 0)),
            scratch_shapes=[
                pltpu.VMEM((heads, 1, rows), jnp.float32),
                pltpu.VMEM((heads, 1, rows), jnp.float32),
                pltpu.VMEM((heads, HD, rows), jnp.float32),
            ],
        ),
        compiler_params=pltpu.CompilerParams(vmem_limit_bytes=56 * 1024 * 1024),
        cost_estimate=pl.CostEstimate(
            flops=4 * pairs * HD,
            bytes_accessed=gathered.size * 2 + 4 * rows * width,
            transcendentals=pairs,
        ),
    )(order, count, queries, gathered, gathered, mark)


def per_device(hidden, queries, key_rows, values, out_weight, level_table, noise_level, group_live):
    rows, width = queries.shape
    out_width = hidden.shape[1]
    groups = lax.axis_size("slot")
    shards = lax.axis_size("tp")
    own_slot = lax.axis_index("slot")
    own_shard = lax.axis_index("tp")
    group = lax.rem(own_slot + 1, groups)

    heads = width // HD
    cut = (heads - max(1, heads // 6)) * HD

    def joined(low, high):
        return jnp.concatenate([key_rows[:, low:high], values[:, low:high]], axis=1)

    first = lax.all_gather(joined(0, cut), "slot", axis=0, tiled=True)
    first_mark = first[:16, :HD]
    level = passed_along(noise_level, "slot", -1)
    queries = passed_along(queries, "slot", -1)

    half = width // 2
    parity = lax.rem(own_slot, 2)
    own_weight = lax.dynamic_slice(out_weight, (0, own_shard * out_width), (width, out_width))
    weights = [own_weight]
    for shift in range(1, shards):
        target = lax.rem(own_shard + shift, shards)
        sent = lax.dynamic_slice(
            out_weight, (parity * half, target * out_width), (half, out_width)
        )
        mine = passed_along(sent, "tp", shift)
        mine, queries, level = lax.optimization_barrier((mine, queries, level))
        other = swapped_with_pair(mine)
        weights.append(
            jnp.concatenate(
                [jnp.where(parity == 0, mine, other), jnp.where(parity == 0, other, mine)], axis=0
            )
        )
    first_weight = jnp.concatenate([own_weight] + [weight[:cut] for weight in weights[1:]], axis=0)
    second_weight = jnp.concatenate([weight[cut:] for weight in weights[1:]], axis=0)
    piece, first_mark, queries, first_weight, second_weight = lax.optimization_barrier(
        (joined(cut, width), first_mark, queries, first_weight, second_weight)
    )
    second = lax.all_gather(piece, "slot", axis=0, tiled=True)
    second_mark = second[:16, :HD]

    slot_ids = jnp.arange(groups, dtype=jnp.int32)
    needed = ((slot_ids < group) & (group_live == 1)) | (slot_ids == group)
    place = jnp.cumsum(needed.astype(jnp.int32)) - 1
    count = jnp.sum(needed.astype(jnp.int32))
    hits = needed[None, :] & (place[None, :] == slot_ids[:, None])
    order = jnp.where(
        slot_ids < count, jnp.sum(jnp.where(hits, slot_ids[None, :], 0), axis=1), group
    ).astype(jnp.int32)
    count = count.reshape(1)

    def from_others(attended):
        return [passed_along(attended, "tp", shift) for shift in range(1, shards)]

    picked = jnp.arange(level_table.shape[0], dtype=jnp.int32) == level[0]
    gate_row = jnp.sum(jnp.where(picked[:, None], level_table, 0.0), axis=0)

    attended = attend(order, count, queries[:, :cut], first, first_mark, groups)
    attended, queries, gate_row = lax.optimization_barrier((attended, queries, gate_row))
    received = from_others(attended)
    second_mark, hidden, received = lax.optimization_barrier((second_mark, hidden, received))
    hidden = passed_along(hidden, "slot", -1)
    last = attend(order, count, queries[:, cut:], second, second_mark, groups)
    last_received = from_others(last)
    projected = jnp.dot(
        jnp.concatenate([attended, last] + received, axis=1),
        first_weight,
        preferred_element_type=jnp.float32,
    )
    projected, last_received = lax.optimization_barrier((projected, last_received))
    projected = projected + jnp.dot(
        jnp.concatenate(last_received, axis=1), second_weight, preferred_element_type=jnp.float32
    )
    return (hidden.astype(jnp.float32) + gate_row[None, :] * projected).astype(jnp.bfloat16)


def solution(mesh):
    in_specs = (
        P("slot", "tp"),
        P("slot", "tp"),
        P("slot", "tp"),
        P("slot", "tp"),
        P("tp", None),
        P(None, "tp"),
        P("slot"),
        P(),
    )
    out_specs = P("slot", "tp")
    return jax.shard_map(
        per_device, mesh=mesh, in_specs=in_specs, out_specs=out_specs, check_vma=False
    )
```
